128 devices in a mesh: replica: 8 (over x_lo, y), fsdp: 16 (over z, x_hi, core).
Axes of the slice: x: 4 (x_hi: 2, x_lo: 2; x = x_hi * 2 + x_lo), y: 4, z: 4, core: 2. Of those that a mesh axis runs over, the one named last changes fastest.
Arguments:
- tokens: bfloat16 [8, 16384, 4096], P('replica', 'fsdp'), may hold values from -6 to 6
- norm_gain: float32 [4096], replicated, may hold values from 0.25 to 1.75
- value_weight: bfloat16 [8, 4096, 512], P('replica', 'fsdp'), may hold values from -0.09375 to 0.09375
- output_weight: bfloat16 [8, 4096, 512], P('replica', 'fsdp'), may hold values from -0.25 to 0.25
- out_cotangent: bfloat16 [8, 16384, 4096], P('replica', 'fsdp'), may hold values from -0.15625 to 0.15625
- base_params: bfloat16 [65536, 128], P('fsdp'), may hold values from -6 to 6
- outer_momentum: float32 [65536, 128], P('fsdp'), may hold values from -4 to 4
- delta_values: bfloat16 [8, 65536, 128], P('replica', 'fsdp'), may hold values from -8 to 8
- delta_exponents: int32 [8, 65536], P('replica', 'fsdp'), may hold values from -3 to 1
Outputs:
- value_grad: float32 [8, 4096, 512], P('replica', 'fsdp')
- output_grad: float32 [8, 4096, 512], P('replica', 'fsdp')
- new_base: bfloat16 [65536, 128], P('fsdp')
- new_momentum: float32 [65536, 128], P('fsdp')
The draws below stay inside these ranges and needn't reach their ends.
All inputs are finite; a program needn't handle non-finite values.
Results may differ from the reference program's by a relative error of at most 0.015.
Values may be sent and summed in bfloat16 or wider, within the bound.
A program may use at most 128 MiB of HBM per device.

```python
import jax
import jax.numpy as jnp
from jax import lax

D = 4096
KV = 512
TOK_DEV = 1024
FRAG_ROWS = 65536
TOKENS = 16384
N_REPLICA = 8
N_FSDP = 16


def place_ends(drawn, rng, least, top_value):
    longest = drawn.shape.index(max(drawn.shape))
    spots = []
    for shift in (0, 1):
        where = [jax.random.randint(jax.random.fold_in(rng, axis), (), 0, length) for axis, length in enumerate(drawn.shape)]
        where[longest] = (where[longest] + shift) % drawn.shape[longest]
        spots.append(tuple(where))
    return drawn.at[spots[0]].set(least).at[spots[1]].set(top_value)


def raised(result, stream_key, source, target, parts, factor):
    owner, partner = [(jnp.arange(result.shape[axis_at]) // (result.shape[axis_at] // parts)).reshape([-1 if axis == axis_at else 1 for axis in range(result.ndim)]) for axis_at in (source, target)]
    chosen = jax.random.permutation(stream_key, parts)[partner]
    strong = (owner == chosen) | (owner == (partner + parts // 2) % parts)
    return jnp.where(strong, factor * result, result)


def shard_levels(key, dims, shards, smallest, largest):
    def one(axis_at, blocks):
        steps = jax.random.uniform(jax.random.fold_in(jax.random.fold_in(key, 6), axis_at), (blocks,), jnp.float32, smallest / len(shards), largest / len(shards))
        return jnp.repeat(jnp.exp(steps), dims[axis_at] // blocks).reshape((-1,) + (1,) * (len(dims) - axis_at - 1))

    level = one(*shards[0])
    for cut in shards[1:]:
        level = level * one(*cut)
    return level


def noise(stream_key, dims, spread, limit, pieces=(), held_as=jnp.bfloat16):
    factor_of = shard_levels(stream_key, dims, pieces, -0.22, 0.18) if pieces else 1.0
    values = jax.random.normal(stream_key, dims, jnp.float32) * spread * factor_of
    return jnp.minimum(jnp.maximum(values, -limit), limit).astype(held_as)


def heavy_noise(rng, shape, scale, bound, cuts, heavy, dtype=jnp.bfloat16):
    drawn = scale * jax.random.normal(rng, shape, jnp.float32)
    if cuts:
        drawn = drawn * shard_levels(rng, shape, cuts, -0.22, 0.18)
    return jnp.clip(raised(drawn, jax.random.fold_in(rng, 3), *heavy), -bound, bound).astype(dtype)


def setup_inputs(seed: int = 0) -> dict:
    keys = jax.random.split(jax.random.key(seed), 10)
    tokens = noise(keys[0], (N_REPLICA, TOKENS, D), 1.0, 6.0, ((0, 8), (1, 16)))
    norm_gain = jnp.clip(1.0 + 0.15 * jax.random.normal(keys[1], (D,), jnp.float32), 0.25, 1.75)
    value_weight = noise(keys[2], (N_REPLICA, D, KV), D ** -0.5, 0.09375, ((0, 8), (1, 16)))
    output_weight = noise(keys[3], (N_REPLICA, D, KV), KV ** -0.5, 0.25, ((0, 8), (1, 16)))
    out_cotangent = heavy_noise(keys[4], (N_REPLICA, TOKENS, D), (TOKENS ** -0.5), 0.15625, ((0, 8), (1, 16)), (1, 2, 16, 2.0))
    base_params = noise(keys[5], (FRAG_ROWS, 128), 1.0, 6.0, ((0, 16),))
    outer_momentum = noise(keys[6], (FRAG_ROWS, 128), 0.5, 4.0, ((0, 16),), jnp.float32)
    delta_values = noise(keys[7], (N_REPLICA, FRAG_ROWS, 128), 1.0, 8.0, ((0, 8), (1, 16)))
    delta_exponents = place_ends(jax.random.randint(keys[8], (N_REPLICA, FRAG_ROWS), -3, 2), jax.random.fold_in(keys[8], 1), -3, 1).astype(jnp.int32)
    return {"tokens": tokens, "norm_gain": norm_gain, "value_weight": value_weight, "output_weight": output_weight, "out_cotangent": out_cotangent, "base_params": base_params, "outer_momentum": outer_momentum, "delta_values": delta_values, "delta_exponents": delta_exponents}


def group_terms(left, right):
    left_groups = left.reshape(N_FSDP, TOK_DEV, left.shape[1])
    right_groups = right.reshape(N_FSDP, TOK_DEV, right.shape[1])

    def one_group(pair):
        term = lax.dot_general(pair[0], pair[1], (((0,), (0,)), ((), ())), preferred_element_type=jnp.float32)
        return term.astype(jnp.bfloat16).astype(jnp.float32)
    terms = lax.map(one_group, (left_groups, right_groups))
    return lax.optimization_barrier(jnp.sum(terms, axis=0))

def replica_grads(tokens_one, gain, value_w, output_w, cotangent):
    xf = tokens_one.astype(jnp.float32)
    scale = lax.rsqrt(lax.optimization_barrier(jnp.mean(xf * xf, axis=1, keepdims=True)) + 1e-05)
    normed = (xf * scale * gain).astype(jnp.bfloat16)
    values = jnp.dot(normed, value_w, preferred_element_type=jnp.float32).astype(jnp.bfloat16)
    value_cot = jnp.dot(cotangent, output_w, preferred_element_type=jnp.float32).astype(jnp.bfloat16)
    output_grad = group_terms(cotangent, values)
    value_grad = group_terms(normed, value_cot)
    return (value_grad, output_grad)

def reference(tokens, norm_gain, value_weight, output_weight, out_cotangent, base_params, outer_momentum, delta_values, delta_exponents):
    value_list = []
    output_list = []
    for index in range(N_REPLICA):
        value_grad, output_grad = replica_grads(tokens[index], norm_gain, value_weight[index], output_weight[index], out_cotangent[index])
        value_list.append(value_grad)
        output_list.append(output_grad)
    scaled = delta_values.astype(jnp.float32) * jnp.exp2(delta_exponents.astype(jnp.float32))[:, :, None]
    delta = lax.optimization_barrier(jnp.sum(scaled, axis=0)) * (1.0 / N_REPLICA)
    new_momentum = 0.9 * outer_momentum + delta
    new_base = (base_params.astype(jnp.float32) - 0.7 * (delta + 0.9 * new_momentum)).astype(jnp.bfloat16)
    return (jnp.stack(value_list), jnp.stack(output_list), new_base, new_momentum)
```

```python
import functools

import jax
import jax.numpy as jnp
from jax import lax
from jax.experimental import pallas as pl
from jax.experimental.pallas import tpu as pltpu
from jax.sharding import PartitionSpec as P

MESH = pl.DeviceIdType.MESH
F32, BF16 = jnp.float32, jnp.bfloat16
WIDTH, KV, TOK, BLOCK = 4096, 512, 1024, 256
FRAG = 4096
SEG = FRAG // 4
W_CUT = (80, 64, 48, 64)
G_CUT = (144, 144, 112, 112)


def parts(cut):
    a0, a1, b0, b1 = cut
    a, b = a0 + a1, b0 + b1
    return {
        "A0": (0, a0),
        "A1": (a0, a1),
        "A": (0, a),
        "B0": (a, b0),
        "B1": (a + b0, b1),
        "B": (a, b),
        "all": (0, a + b),
    }


W_PART, G_PART = parts(W_CUT), parts(G_CUT)
GATHER_MSGS = 23
REDUCE_MSGS = 23
V_GATHER, O_GATHER = 0, GATHER_MSGS
O_REDUCE, V_REDUCE = 2 * GATHER_MSGS, 2 * GATHER_MSGS + REDUCE_MSGS
DELTA = 2 * GATHER_MSGS + 2 * REDUCE_MSGS
MSGS = DELTA + 7
TOK_PARTS = 8
TOK_ROWS = TOK // TOK_PARTS


def kernel(
    tok_in,
    gain,
    wv_in,
    wo_in,
    cot_in,
    base_in,
    mom_in,
    dv_in,
    exps,
    vg_out,
    og_out,
    nb_out,
    nm_out,
    normed,
    cot,
    wv,
    wo,
    acc,
    factors,
    partial,
    staged,
    from_core,
    from_x,
    from_z,
    base,
    mom,
    scaled,
    segs,
    seg_own,
    seg_x,
    delta,
    grads,
    send_sem,
    recv_sem,
    load_sem,
    store_sem,
):
    r, f = lax.axis_index("replica"), lax.axis_index("fsdp")
    x_lo, y = r // 4, lax.rem(r, 4)
    z, x, c = f // 4, lax.rem(f // 2, 2), lax.rem(f, 2)
    up, down, far = lax.rem(z + 1, 4), lax.rem(z + 3, 4), lax.rem(z + 2, 4)
    other = 1 - x

    def place(zz, xx):
        return {"fsdp": zz * 4 + xx * 2 + c}

    to_core = {"fsdp": z * 4 + x * 2 + (1 - c)}
    to_x, to_up, to_down = place(z, other), place(up, x), place(down, x)
    to_y = [{"replica": x_lo * 4 + lax.rem(y + k, 4)} for k in (1, 2, 3)]
    to_side = {"replica": (1 - x_lo) * 4 + y}

    sent = []

    def send(k, src, dst, to):
        copy = pltpu.make_async_remote_copy(
            src_ref=src,
            dst_ref=dst,
            send_sem=send_sem.at[k],
            recv_sem=recv_sem.at[k],
            device_id=to,
            device_id_type=MESH,
        )
        copy.start()
        sent.append(copy)

    def arrive(k, dst):
        pltpu.make_async_remote_copy(
            src_ref=dst,
            dst_ref=dst,
            send_sem=send_sem.at[k],
            recv_sem=recv_sem.at[k],
            device_id=to_core,
            device_id_type=MESH,
        ).wait_recv()

    loads = {}

    def load(name, src, dst):
        loads[name] = pltpu.make_async_copy(src, dst, load_sem.at[len(loads)])
        loads[name].start()

    def own_rows(buf, zz, xx, cc, part="all"):
        first, count = W_PART[part]
        start = pl.multiple_of(((zz * 2 + xx) * 2 + cc) * BLOCK + first, 16)
        return buf.at[pl.ds(start, count)]

    load("wv", wv_in.at[0], own_rows(wv, z, x, c))
    load("dv", dv_in.at[0], scaled)
    for k in range(TOK_PARTS):
        rows = pl.ds(k * TOK_ROWS, TOK_ROWS)
        load(("tok", k), tok_in.at[0, rows], normed.at[rows])
    load("wo", wo_in.at[0], own_rows(wo, z, x, c))
    load("cot", cot_in.at[0], cot)
    load("base", base_in, base)
    load("mom", mom_in, mom)

    barrier = pltpu.get_barrier_semaphore()
    partners = [to_core, to_x, to_up, to_down, to_side] + to_y
    for to in partners:
        pl.semaphore_signal(barrier, inc=1, device_id=to, device_id_type=MESH)
    pl.semaphore_wait(barrier, len(partners))

    def gather_start(k0, w_in, buf):
        mine = own_rows(buf, z, x, c)
        send(k0 + 0, w_in.at[0], mine, to_x)
        send(k0 + 1, w_in.at[0], mine, to_up)
        send(k0 + 2, w_in.at[0], mine, to_down)
        send(k0 + 3, w_in.at[0], mine, to_core)

    def gather(k0, buf, left, total, factor, own):
        def rows(zz, xx, part="all"):
            return own_rows(buf, zz, xx, c, part)

        def pass_on(k, zz, xx, part, to):
            piece = rows(zz, xx, part)
            send(k0 + k, piece, piece, to)

        def got(k, zz, xx, part="all"):
            arrive(k0 + k, rows(zz, xx, part))

        def multiply(zz, xx, first=False):
            start = pl.multiple_of((zz * 2 + xx) * 2 * BLOCK, 2 * BLOCK)
            both = pl.ds(start, 2 * BLOCK)

            def tile(m, _):
                at = pl.ds(pl.multiple_of(m * 256, 256), 256)
                term = jnp.dot(left[at, both], buf[both, :], preferred_element_type=F32)
                if first:
                    total[at, :] = term
                else:
                    total[at, :] += term
                return 0

            lax.fori_loop(0, TOK // 256, tile, 0)

        def from_sibling(k, zz, xx):
            arrive(k0 + k, own_rows(buf, zz, xx, 1 - c))

        got(0, z, other)
        pass_on(4, z, other, "A", to_up)
        pass_on(5, z, other, "A", to_down)
        pass_on(16, z, other, "all", to_core)
        yield
        got(1, down, x)
        pass_on(6, down, x, "A0", to_up)
        pass_on(7, down, x, "B0", to_up)
        pass_on(8, down, x, "B", to_x)
        pass_on(17, down, x, "all", to_core)
        yield
        got(2, up, x)
        pass_on(9, up, x, "A1", to_down)
        pass_on(10, up, x, "B1", to_down)
        pass_on(11, up, x, "B", to_x)
        pass_on(18, up, x, "all", to_core)
        yield
        loads[own].wait()
        from_sibling(3, z, x)
        multiply(z, x, first=True)
        yield
        from_sibling(16, z, other)
        multiply(z, other)
        yield
        got(4, down, other, "A")
        pass_on(12, down, other, "A0", to_up)
        got(5, up, other, "A")
        pass_on(13, up, other, "A1", to_down)
        yield
        from_sibling(17, down, x)
        multiply(down, x)
        yield
        got(6, far, x, "A0")
        got(7, far, x, "B0")
        pass_on(14, far, x, "B0", to_x)
        got(9, far, x, "A1")
        got(10, far, x, "B1")
        pass_on(15, far, x, "B1", to_x)
        pass_on(21, far, x, "all", to_core)
        yield
        from_sibling(18, up, x)
        multiply(up, x)
        yield
        got(8, down, other, "B")
        pass_on(19, down, other, "all", to_core)
        got(11, up, other, "B")
        pass_on(20, up, other, "all", to_core)
        yield
        from_sibling(21, far, x)
        multiply(far, x)
        yield
        from_sibling(19, down, other)
        multiply(down, other)
        yield
        from_sibling(20, up, other)
        multiply(up, other)
        yield
        got(12, far, other, "A0")
        got(13, far, other, "A1")
        got(14, far, other, "B0")
        got(15, far, other, "B1")
        pass_on(22, far, other, "all", to_core)
        yield
        from_sibling(22, far, other)
        multiply(far, other)

        def turn(m, _):
            at = pl.ds(pl.multiple_of(m * 256, 256), 256)
            factor[:, at] = total[at, :].T.astype(BF16)
            return 0

        lax.fori_loop(0, TOK // 256, turn, 0)
        yield

    dests = [(far, other), (up, other), (down, other), (z, other), (far, x), (up, x), (down, x), (z, x)]

    def reduce(k0, g, factor, right, out, store):
        mine, stage, core_in = partial.at[g], staged.at[g], from_core.at[g]
        x_in, z_in = from_x.at[g], from_z.at[g]

        def cut(ref, part):
            first, count = G_PART[part]
            return ref.at[pl.ds(first, count)]

        def block(d, cc, into):
            zz, xx = dests[d]
            columns = pl.ds(pl.multiple_of(((zz * 2 + xx) * 2 + cc) * BLOCK, BLOCK), BLOCK)

            def tile(m, _):
                at = pl.ds(pl.multiple_of(m * 256, 256), 256)
                term = jnp.dot(factor[at, :], right[:, columns], preferred_element_type=F32)
                into[d, at, :] = term.astype(BF16)
                return 0

            lax.fori_loop(0, KV // 256, tile, 0)

        def compute(d):
            block(d, 1 - c, stage)
            send(k0 + d, stage.at[d], core_in.at[d], to_core)
            block(d, c, mine)

        def add(to, term, count):
            def some(m, _):
                at = pl.ds(pl.multiple_of(m * 16, 16), 16)
                to[at, :] = (to[at, :].astype(F32) + term[at, :].astype(F32)).astype(BF16)
                return 0

            lax.fori_loop(0, count // 16, some, 0, unroll=True)

        def combine(d):
            arrive(k0 + d, core_in.at[d])
            add(mine.at[d], core_in.at[d], KV)

        def add_part(d, part, k, term):
            arrive(k0 + k, term)
            add(cut(mine.at[d], part), term, G_PART[part][1])

        rows_of = {part: G_PART[part][1] for part in G_PART}
        offset = [0]

        def slot(ref, part):
            start = offset[0]
            offset[0] += rows_of[part]
            return ref.at[pl.ds(start, rows_of[part])]

        land = {}
        for k, part in ((8, "B"), (9, "B"), (10, "B"), (11, "B"), (22, "A")):
            land[k] = slot(x_in, part)
        offset[0] = 0
        for k, part in (
            (12, "A0"), (13, "A1"), (14, "A"), (15, "A"), (16, "A0"), (17, "A1"), (18, "B0"), (19, "B1"), (20, "all"), (21, "all"),
        ):
            land[k] = slot(z_in, part)

        def ship(k, d, part, to):
            send(k0 + k, cut(mine.at[d], part), land[k], to)

        compute(0)
        yield
        compute(1)
        combine(0)
        ship(12, 0, "A0", to_up)
        ship(13, 0, "A1", to_down)
        ship(8, 0, "B", to_x)
        yield
        compute(2)
        combine(1)
        ship(9, 1, "B", to_x)
        yield
        compute(3)
        combine(2)
        ship(10, 2, "B", to_x)
        yield
        add_part(1, "A0", 12, land[12])
        ship(14, 1, "A", to_up)
        add_part(2, "A1", 13, land[13])
        ship(15, 2, "A", to_down)
        yield
        compute(4)
        combine(3)
        ship(11, 3, "B", to_x)
        yield
        compute(5)
        combine(4)
        ship(16, 4, "A0", to_up)
        ship(17, 4, "A1", to_down)
        add_part(4, "B", 8, land[8])
        ship(18, 4, "B0", to_up)
        ship(19, 4, "B1", to_down)
        yield
        compute(6)
        combine(5)
        add_part(5, "B", 9, land[9])
        yield
        compute(7)
        combine(6)
        add_part(6, "B", 10, land[10])
        yield
        add_part(5, "A0", 16, land[16])
        add_part(5, "B0", 18, land[18])
        ship(20, 5, "all", to_up)
        add_part(6, "A1", 17, land[17])
        add_part(6, "B1", 19, land[19])
        ship(21, 6, "all", to_down)
        yield
        combine(7)
        add_part(7, "B", 11, land[11])
        yield
        add_part(3, "A", 14, land[14])
        add_part(3, "A", 15, land[15])
        ship(22, 3, "A", to_x)
        yield
        arrive(k0 + 20, land[20])
        arrive(k0 + 21, land[21])
        add(mine.at[7], land[20], KV)
        add(mine.at[7], land[21], KV)
        yield
        add_part(7, "A", 22, land[22])

        def turn(m, _):
            at = pl.ds(pl.multiple_of(m * 128, 128), 128)
            grads[g, :, at] = mine[7, at, :].astype(F32).T
            return 0

        lax.fori_loop(0, KV // 128, turn, 0)
        pltpu.make_async_copy(grads.at[g], out.at[0], store_sem.at[store]).start()
        yield

    def run(task, steps):
        for _ in range(steps):
            next(task, None)

    def finish(task):
        for _ in task:
            pass

    def seg(buf, k):
        return buf.at[pl.ds(pl.multiple_of(lax.rem(y + k, 4) * SEG, SEG), SEG)]

    def outer_step():
        loads["dv"].wait()

        def scale(m, _):
            at = pl.ds(pl.multiple_of(m * 128, 128), 128)
            factor = jnp.exp2(exps[:, at].astype(F32))
            factor = jnp.broadcast_to(factor, (128, 128)).T
            scaled[at, :] = (scaled[at, :].astype(F32) * factor).astype(BF16)
            return 0

        lax.fori_loop(0, FRAG // 128, scale, 0)
        for k in (1, 2, 3):
            send(DELTA + k - 1, seg(scaled, k), segs.at[k - 1], to_y[k - 1])
        yield
        for k in (1, 2, 3):
            arrive(DELTA + k - 1, segs.at[k - 1])
        first = pl.multiple_of(y * SEG, SEG)

        def total(m, _):
            at = pl.ds(pl.multiple_of(m * 32, 32), 32)
            value = scaled[pl.ds(pl.multiple_of(first + m * 32, 32), 32), :].astype(F32)
            for k in range(3):
                value += segs[k, at, :].astype(F32)
            seg_own[at, :] = value.astype(BF16)
            return 0

        lax.fori_loop(0, SEG // 32, total, 0)
        send(DELTA + 3, seg_own, seg_x, to_side)
        yield
        arrive(DELTA + 3, seg_x)

        def both(m, _):
            at = pl.ds(pl.multiple_of(m * 32, 32), 32)
            value = seg_own[at, :].astype(F32) + seg_x[at, :].astype(F32)
            delta[pl.ds(pl.multiple_of(first + m * 32, 32), 32), :] = value.astype(BF16)
            return 0

        lax.fori_loop(0, SEG // 32, both, 0)
        for k in (1, 2, 3):
            send(DELTA + 3 + k, seg(delta, 0), seg(delta, 0), to_y[k - 1])
        yield
        for k in (1, 2, 3):
            arrive(DELTA + 3 + k, seg(delta, 4 - k))
        loads["base"].wait()
        loads["mom"].wait()

        def update(m, _):
            at = pl.ds(pl.multiple_of(m * 64, 64), 64)
            mean = delta[at, :].astype(F32) * 0.125
            new = 0.9 * mom[at, :] + mean
            mom[at, :] = new
            base[at, :] = (base[at, :].astype(F32) - 0.7 * (mean + 0.9 * new)).astype(BF16)
            return 0

        lax.fori_loop(0, FRAG // 64, update, 0)
        pltpu.make_async_copy(base, nb_out, store_sem.at[2]).start()
        pltpu.make_async_copy(mom, nm_out, store_sem.at[3]).start()
        yield

    gather_v = gather(V_GATHER, wv, normed, acc.at[0], factors.at[0], "wv")
    gather_o = gather(O_GATHER, wo, cot, acc.at[1], factors.at[1], "wo")
    reduce_o = reduce(O_REDUCE, 0, factors.at[0], cot, og_out, 0)
    reduce_v = reduce(V_REDUCE, 1, factors.at[1], normed, vg_out, 1)
    outer = outer_step()

    gather_start(V_GATHER, wv_in, wv)
    run(outer, 1)

    for k in range(TOK_PARTS):
        loads[("tok", k)].wait()

        def norm(m, _):
            at = pl.ds(pl.multiple_of(k * TOK_ROWS + m * 16, 16), 16)
            value = normed[at, :].astype(F32)
            scale = lax.rsqrt(jnp.mean(value * value, axis=1, keepdims=True) + 1e-05)
            normed[at, :] = (value * scale * gain[...]).astype(BF16)
            return 0

        lax.fori_loop(0, TOK_ROWS // 16, norm, 0)

    gather_start(O_GATHER, wo_in, wo)
    run(gather_v, 5)
    run(outer, 1)
    loads["cot"].wait()
    run(gather_o, 3)
    run(gather_v, 20)
    for _ in range(6):
        run(gather_o, 2)
        run(reduce_o, 1)
        run(outer, 1)
    run(gather_o, 20)
    run(reduce_o, 3)
    for _ in range(4):
        run(reduce_v, 2)
        run(reduce_o, 1)
    finish(reduce_o)
    finish(reduce_v)
    finish(outer)
    for copy in sent:
        copy.wait_send()
    for src, dst, k in (
        (grads.at[0], og_out.at[0], 0),
        (grads.at[1], vg_out.at[0], 1),
        (base, nb_out, 2),
        (mom, nm_out, 3),
    ):
        pltpu.make_async_copy(src, dst, store_sem.at[k]).wait()


def per_device(tokens, gain, value_w, output_w, cotangent, base, momentum, delta_values, exps):
    any_place, vmem = pl.BlockSpec(memory_space=pl.ANY), pl.BlockSpec(memory_space=pltpu.VMEM)
    grad_x = 4 * G_PART["B"][1] + G_PART["A"][1]
    grad_z = 6 * KV - 3 * G_PART["B"][1]
    return pl.pallas_call(
        kernel,
        out_shape=(
            jax.ShapeDtypeStruct((1, BLOCK, KV), F32),
            jax.ShapeDtypeStruct((1, BLOCK, KV), F32),
            jax.ShapeDtypeStruct((FRAG, 128), BF16),
            jax.ShapeDtypeStruct((FRAG, 128), F32),
        ),
        in_specs=[any_place, vmem, any_place, any_place, any_place, any_place, any_place, any_place, vmem],
        out_specs=(any_place,) * 4,
        scratch_shapes=[
            pltpu.VMEM((TOK, WIDTH), BF16),
            pltpu.VMEM((TOK, WIDTH), BF16),
            pltpu.VMEM((WIDTH, KV), BF16),
            pltpu.VMEM((WIDTH, KV), BF16),
            pltpu.VMEM((2, TOK, KV), F32),
            pltpu.VMEM((2, KV, TOK), BF16),
            pltpu.VMEM((2, 8, KV, BLOCK), BF16),
            pltpu.VMEM((2, 8, KV, BLOCK), BF16),
            pltpu.VMEM((2, 8, KV, BLOCK), BF16),
            pltpu.VMEM((2, grad_x, BLOCK), BF16),
            pltpu.VMEM((2, grad_z, BLOCK), BF16),
            pltpu.VMEM((FRAG, 128), BF16),
            pltpu.VMEM((FRAG, 128), F32),
            pltpu.VMEM((FRAG, 128), BF16),
            pltpu.VMEM((3, SEG, 128), BF16),
            pltpu.VMEM((SEG, 128), BF16),
            pltpu.VMEM((SEG, 128), BF16),
            pltpu.VMEM((FRAG, 128), BF16),
            pltpu.VMEM((2, BLOCK, KV), F32),
            pltpu.SemaphoreType.DMA((MSGS,)),
            pltpu.SemaphoreType.DMA((MSGS,)),
            pltpu.SemaphoreType.DMA((TOK_PARTS + 6,)),
            pltpu.SemaphoreType.DMA((4,)),
        ],
        compiler_params=pltpu.CompilerParams(
            collective_id=0, has_side_effects=True, vmem_limit_bytes=60 * 2**20
        ),
        name="layer_and_outer_step",
    )(tokens, gain.reshape(1, WIDTH), value_w, output_w, cotangent, base, momentum, delta_values, exps)


def solution(mesh):
    return jax.shard_map(
        per_device,
        mesh=mesh,
        in_specs=(
            P("replica", "fsdp", None),
            P(),
            P("replica", "fsdp", None),
            P("replica", "fsdp", None),
            P("replica", "fsdp", None),
            P("fsdp", None),
            P("fsdp", None),
            P("replica", "fsdp", None),
            P("replica", "fsdp"),
        ),
        out_specs=(
            P("replica", "fsdp", None),
            P("replica", "fsdp", None),
            P("fsdp", None),
            P("fsdp", None),
        ),
        check_vma=False,
    )
```

```python
import jax
import jax.numpy as jnp
from jax import lax
from jax.experimental import pallas as pl
from jax.experimental.pallas import tpu as pltpu
from jax.sharding import PartitionSpec as P

MESH = pl.DeviceIdType.MESH
F32, BF16 = jnp.float32, jnp.bfloat16
WIDTH, KV, TOK, BLOCK = 4096, 512, 1024, 256
FRAG = 4096
SEG = FRAG // 4
NORM_ROWS = 64
TOK_PARTS = 8
UPDATES = 4

CUTS = ({"A0": 80, "A1": 80, "B0": 48, "B1": 48},) * 2


def plan():
    found = []

    def send(link, block, part, cause):
        dz, dx = block
        lands = {"U": ((dz + 3) % 4, dx), "D": ((dz + 1) % 4, dx), "S": (dz, 1 - dx)}[link]
        found.append((link, block, lands, part, cause))

    for part in ("A0", "A1", "B0", "B1"):
        send("S", (0, 0), part, None)
    for part in ("A0", "B0", "B1", "A1"):
        send("U", (0, 0), part, None)
    for part in ("A1", "B1", "B0", "A0"):
        send("D", (0, 0), part, None)
    k = 0
    while k < len(found):
        link, _, at, part, _ = found[k]
        if at == (0, 1) and part in ("A0", "A1"):
            send("U", at, part, k)
            send("D", at, part, k)
        if at in ((3, 0), (3, 1)) and link == "U" and part in ("A0", "B0"):
            send("U", at, part, k)
        if at in ((1, 0), (1, 1)) and link == "D" and part in ("A1", "B1"):
            send("D", at, part, k)
        if at[1] == 0 and link != "S" and part in ("B0", "B1"):
            send("S", at, part, k)
        k += 1
    return found


PLAN = plan()
CHILDREN = [[c for c, m in enumerate(PLAN) if m[4] == k] for k in range(len(PLAN))]
BLOCKS = [(dz, dx) for dx in (1, 0) for dz in (2, 1, 3, 0)]
COUNT = len(PLAN)
GROUP = COUNT + len(BLOCKS)
DELTA = 4 * GROUP
MSGS = DELTA + 7
BACK = {"U": "D", "D": "U", "S": "S"}
ORDER = (
    ("start", 0, 0), ("scale", 0, 0), ("mul", 0, 7), ("norm", 0, 0), ("norm", 0, 1), ("rx", 0, 4), ("rx", 0, 8),
    ("norm", 0, 2), ("norm", 0, 3), ("rx", 0, 0), ("norm", 0, 4), ("rx", 0, 5), ("rx", 0, 9), ("norm", 0, 5),
    ("norm", 0, 6), ("norm", 0, 7), ("rx", 0, 6), ("rx", 0, 10), ("rx", 0, 1), ("start", 1, 0), ("norm", 0, 8),
    ("norm", 0, 9), ("rx", 0, 2), ("norm", 0, 10), ("rx", 0, 7), ("rx", 0, 11), ("norm", 0, 11), ("norm", 0, 12),
    ("rx", 0, 3), ("norm", 0, 13), ("norm", 0, 14), ("norm", 0, 15), ("rx", 0, 18), ("rx", 0, 16), ("rx", 0, 20),
    ("mul", 1, 7), ("mul", 0, 6), ("rx", 0, 22), ("mul", 0, 5), ("rx", 0, 12), ("rx", 0, 13), ("rx", 0, 19),
    ("mul", 0, 3), ("rx", 0, 17), ("rx", 0, 21), ("rx", 0, 23), ("rx", 0, 14), ("rx", 0, 15), ("rx", 1, 0),
    ("dsum", 0, 0), ("mul", 0, 4), ("rx", 1, 4), ("rx", 1, 8), ("rx", 1, 1), ("mul", 0, 2), ("rx", 1, 5), ("rx", 1, 9),
    ("rx", 1, 2), ("mul", 0, 1), ("rx", 1, 6), ("rx", 1, 10), ("rx", 1, 3), ("rx", 0, 26), ("rx", 1, 7), ("rx", 1, 11),
    ("rx", 0, 27), ("mul", 1, 3), ("rx", 0, 24), ("rx", 0, 25), ("mul", 1, 6), ("mul", 1, 5), ("rx", 1, 12),
    ("rx", 1, 13), ("mul", 0, 0), ("blk", 0, 0), ("rx", 1, 16), ("rx", 1, 20), ("blk", 0, 1), ("dboth", 0, 0),
    ("blk", 0, 2), ("rx", 1, 15), ("rx", 1, 14), ("rx", 1, 18), ("blk", 0, 3), ("rx", 1, 17), ("rx", 1, 21),
    ("rx", 1, 22), ("cmb", 0, 0), ("cmb", 0, 1), ("blk", 0, 4), ("rx", 1, 19), ("rx", 1, 24), ("cmb", 0, 2),
    ("rx", 1, 23), ("blk", 0, 5), ("cmb", 0, 3), ("rx", 1, 25), ("blk", 0, 6), ("rx", 1, 26), ("cmb", 0, 4),
    ("blk", 0, 7), ("rx", 1, 27), ("snd", 0, 15), ("snd", 0, 12), ("mul", 1, 4), ("snd", 0, 17), ("cmb", 0, 5),
    ("mul", 1, 2), ("snd", 0, 21), ("cmb", 0, 6), ("mul", 1, 1), ("cmb", 0, 7), ("snd", 0, 4), ("snd", 0, 8),
    ("mul", 1, 0), ("snd", 0, 10), ("blk", 1, 0), ("snd", 0, 0), ("snd", 0, 1), ("blk", 1, 1), ("snd", 0, 5),
    ("snd", 0, 6), ("blk", 1, 2), ("blk", 1, 3), ("snd", 0, 9), ("cmb", 1, 0), ("cmb", 1, 1), ("blk", 1, 4),
    ("cmb", 1, 2), ("blk", 1, 5), ("cmb", 1, 3), ("blk", 1, 6), ("blk", 1, 7), ("cmb", 1, 4), ("snd", 1, 17),
    ("snd", 1, 12), ("snd", 1, 15), ("cmb", 1, 5), ("snd", 1, 21), ("fin", 0, 0), ("fin", 0, 2), ("fin", 0, 3),
    ("fin", 0, 1), ("cmb", 1, 6), ("upd", 0, 0), ("cmb", 1, 7), ("upd", 0, 1), ("snd", 1, 10), ("upd", 0, 2),
    ("upd", 0, 3), ("snd", 1, 4), ("snd", 1, 8), ("snd", 1, 6), ("snd", 1, 5), ("snd", 1, 1), ("snd", 1, 0),
    ("snd", 1, 9), ("fin", 1, 1), ("fin", 1, 2), ("fin", 1, 3), ("fin", 1, 0),
)


def kernel(
    tok_in,
    gain,
    wv_in,
    wo_in,
    cot_in,
    base_in,
    mom_in,
    dv_in,
    exps,
    vg_out,
    og_out,
    base,
    mom,
    normed,
    cot,
    wv,
    wo,
    acc,
    factors,
    partial,
    from_core,
    landed,
    scaled,
    segs,
    seg_own,
    seg_x,
    delta,
    send_sem,
    recv_sem,
    load_sem,
):
    r, f = lax.axis_index("replica"), lax.axis_index("fsdp")
    x_lo, y = r // 4, lax.rem(r, 4)
    z, x, c = f // 4, lax.rem(f // 2, 2), lax.rem(f, 2)

    def chip(block):
        dz, dx = block
        return lax.rem(z + dz, 4) * 2 + (1 - x if dx else x)

    to_core = {"fsdp": chip((0, 0)) * 2 + 1 - c}
    to = {"U": {"fsdp": chip((1, 0)) * 2 + c}, "D": {"fsdp": chip((3, 0)) * 2 + c}, "S": {"fsdp": chip((0, 1)) * 2 + c}}
    to_y = [{"replica": x_lo * 4 + lax.rem(y + k, 4)} for k in (1, 2, 3)]
    to_side = {"replica": (1 - x_lo) * 4 + y}

    sent = []

    def copy_of(k, src, dst, device):
        return pltpu.make_async_remote_copy(
            src_ref=src,
            dst_ref=dst,
            send_sem=send_sem.at[k],
            recv_sem=recv_sem.at[k],
            device_id=device,
            device_id_type=MESH,
        )

    def send(k, src, dst, device):
        sent.append(copy_of(k, src, dst, device))
        sent[-1].start()

    def arrive(k, dst):
        copy_of(k, dst, dst, to_core).wait_recv()

    loads, waited = {}, set()

    def load(name, src, dst):
        loads[name] = pltpu.make_async_copy(src, dst, load_sem.at[len(loads)])
        loads[name].start()

    def loaded(name):
        if name not in waited:
            waited.add(name)
            loads[name].wait()

    weights, weights_in = (wo, wv), (wo_in, wv_in)
    left, right, outs = (cot, normed), (normed, cot), (vg_out, og_out)

    def rows_of(g, part):
        cut = CUTS[g]
        first = 0
        for name in ("A0", "A1", "B0", "B1"):
            if name == part:
                return first, cut[name]
            first += cut[name]
        return 0, BLOCK

    def weight(g, block, core, part=None):
        first, count = rows_of(g, part)
        return weights[g].at[pl.ds(pl.multiple_of((chip(block) * 2 + core) * BLOCK + first, 16), count)]

    barrier = pltpu.get_barrier_semaphore()
    partners = [to_core, to["U"], to["D"], to["S"], to_side] + to_y
    for device in partners:
        pl.semaphore_signal(barrier, inc=1, device_id=device, device_id_type=MESH)
    pl.semaphore_wait(barrier, len(partners))

    load("own0", wo_in.at[0], weight(0, (0, 0), c))
    load("own1", wv_in.at[0], weight(1, (0, 0), c))

    def load_rest():
        load("dv", dv_in.at[0], scaled)
        load("cot", cot_in.at[0], cot)
        for k in range(TOK_PARTS):
            rows = pl.ds(k * (TOK // TOK_PARTS), TOK // TOK_PARTS)
            load(("tok", k), tok_in.at[0, rows], normed.at[rows])
        load("base", base_in, base)
        load("mom", mom_in, mom)

    received = {}
    multiplied = [0, 0]

    def start(g, _):
        own = {link: [k for k, m in enumerate(PLAN) if m[4] is None and m[0] == link] for link in "SUD"}
        for i in range(4):
            for link in "SUD":
                k = own[link][i]
                first, count = rows_of(g, PLAN[k][3])
                piece = weights_in[g].at[0, pl.ds(first, count)]
                send(g * GROUP + k, piece, weight(g, (0, 0), c, PLAN[k][3]), to[link])
        send(g * GROUP + COUNT + BLOCKS.index((0, 0)), weights_in[g].at[0], weight(g, (0, 0), c), to_core)

    def rx(g, k):
        _, _, block, part, _ = PLAN[k]
        piece = weight(g, block, c, part)
        arrive(g * GROUP + k, piece)
        for child in CHILDREN[k]:
            send(g * GROUP + child, piece, piece, to[PLAN[child][0]])
        received[g, block] = received.get((g, block), 0) + 1
        if received[g, block] == 4:
            whole = weight(g, block, c)
            send(g * GROUP + COUNT + BLOCKS.index(block), whole, whole, to_core)

    def mul(g, b):
        block = BLOCKS[b]
        if block == (0, 0):
            loaded("own%d" % g)
        if g == 0:
            loaded("cot")
        arrive(g * GROUP + COUNT + b, weight(g, block, 1 - c))
        both = pl.ds(pl.multiple_of(chip(block) * 2 * BLOCK, 2 * BLOCK), 2 * BLOCK)
        term = jnp.dot(left[g][:, both], weights[g][both, :], preferred_element_type=F32)
        multiplied[g] += 1
        if multiplied[g] == 1:
            acc[g] = term
        elif multiplied[g] < len(BLOCKS):
            acc[g] += term
        else:
            factors[g] = (acc[g] + term).astype(BF16)

    def mine(g, b, part=None):
        first, count = rows_of(g, part)
        return partial.at[g, b, pl.ds(pl.multiple_of(c * BLOCK + first, 16), count)]

    def slot(g, k):
        first = sum(CUTS[g][m[3]] for m in PLAN[:k])
        return landed.at[g, pl.ds(first, CUTS[g][PLAN[k][3]])]

    def add(ref, term):
        ref[...] = (ref[...].astype(F32) + term[...].astype(F32)).astype(BF16)

    def blk(g, b):
        columns = pl.ds(pl.multiple_of(chip(BLOCKS[b]) * 2 * BLOCK, 2 * BLOCK), 2 * BLOCK)
        term = lax.dot_general(right[g][:, columns], factors[g], (((0,), (0,)), ((), ())), preferred_element_type=F32)
        partial[g, b] = term.astype(BF16)
        theirs = partial.at[g, b, pl.ds(pl.multiple_of((1 - c) * BLOCK, BLOCK), BLOCK)]
        send((2 + g) * GROUP + COUNT + b, theirs, from_core.at[g, b], to_core)

    def ship(g, k):
        link, _, block, part, _ = PLAN[k]
        send((2 + g) * GROUP + k, mine(g, BLOCKS.index(block), part), slot(g, k), to[BACK[link]])

    def cmb(g, b):
        arrive((2 + g) * GROUP + COUNT + b, from_core.at[g, b])
        add(mine(g, b), from_core.at[g, b])
        for k, m in enumerate(PLAN):
            if m[2] == BLOCKS[b] and not CHILDREN[k]:
                ship(g, k)

    def snd(g, k):
        piece = mine(g, BLOCKS.index(PLAN[k][2]), PLAN[k][3])
        for child in CHILDREN[k]:
            arrive((2 + g) * GROUP + child, slot(g, child))
            add(piece, slot(g, child))
        ship(g, k)

    def fin(g, i):
        part = ("A0", "A1", "B0", "B1")[i]
        first, count = rows_of(g, part)
        total = mine(g, BLOCKS.index((0, 0)), part)[...].astype(F32)
        for k, m in enumerate(PLAN):
            if m[4] is None and m[3] == part:
                arrive((2 + g) * GROUP + k, slot(g, k))
                total += slot(g, k)[...].astype(F32)
        outs[g][0, pl.ds(first, count), :] = total

    def norm(_, i):
        loaded(("tok", i * NORM_ROWS // (TOK // TOK_PARTS)))
        at = pl.ds(i * NORM_ROWS, NORM_ROWS)
        value = normed[at, :].astype(F32)
        scale = lax.rsqrt(jnp.mean(value * value, axis=1, keepdims=True) + 1e-05)
        normed[at, :] = (value * scale * gain[...]).astype(BF16)

    def seg(buf, k):
        return buf.at[pl.ds(pl.multiple_of(lax.rem(y + k, 4) * SEG, SEG), SEG)]

    def scale(_, __):
        loaded("dv")

        def some(m, _):
            at = pl.ds(pl.multiple_of(m * 128, 128), 128)
            factor = jnp.exp2(exps[:, at].astype(F32))
            factor = jnp.broadcast_to(factor, (128, 128)).T
            scaled[at, :] = (scaled[at, :].astype(F32) * factor).astype(BF16)
            return 0

        lax.fori_loop(0, FRAG // 128, some, 0, unroll=4)
        for k in (1, 2, 3):
            send(DELTA + k - 1, seg(scaled, k), segs.at[k - 1], to_y[k - 1])

    def dsum(_, __):
        for k in (1, 2, 3):
            arrive(DELTA + k - 1, segs.at[k - 1])

        def some(m, _):
            at = pl.ds(pl.multiple_of(m * 128, 128), 128)
            value = scaled[pl.ds(pl.multiple_of(y * SEG + m * 128, 128), 128), :].astype(F32)
            for k in range(3):
                value += segs[k, at, :].astype(F32)
            seg_own[at, :] = value.astype(BF16)
            return 0

        lax.fori_loop(0, SEG // 128, some, 0)
        send(DELTA + 3, seg_own, seg_x, to_side)

    def dboth(_, __):
        arrive(DELTA + 3, seg_x)

        def some(m, _):
            at = pl.ds(pl.multiple_of(m * 128, 128), 128)
            value = seg_own[at, :].astype(F32) + seg_x[at, :].astype(F32)
            delta[pl.ds(pl.multiple_of(y * SEG + m * 128, 128), 128), :] = value.astype(BF16)
            return 0

        lax.fori_loop(0, SEG // 128, some, 0)
        for k in (1, 2, 3):
            send(DELTA + 3 + k, seg(delta, 0), seg(delta, 0), to_y[k - 1])

    def upd(_, i):
        if i == 0:
            for k in (1, 2, 3):
                arrive(DELTA + 3 + k, seg(delta, 4 - k))
            loaded("base")
            loaded("mom")

        def some(m, _):
            at = pl.ds(pl.multiple_of(i * (FRAG // UPDATES) + m * 128, 128), 128)
            mean = delta[at, :].astype(F32) * 0.125
            new = 0.9 * mom[at, :] + mean
            mom[at, :] = new
            base[at, :] = (base[at, :].astype(F32) - 0.7 * (mean + 0.9 * new)).astype(BF16)
            return 0

        lax.fori_loop(0, FRAG // UPDATES // 128, some, 0)

    tasks = {
        "start": start,
        "rx": rx,
        "mul": mul,
        "blk": blk,
        "cmb": cmb,
        "snd": snd,
        "fin": fin,
        "norm": norm,
        "scale": scale,
        "dsum": dsum,
        "dboth": dboth,
        "upd": upd,
    }
    for name, g, k in ORDER:
        tasks[name](g, k)
        if (name, g) == ("start", 0):
            load_rest()
    for copy in sent:
        copy.wait_send()


def hand_over(*refs):
    sem = refs[-1]
    arrays = (len(refs) - 1) // 2
    copies = [pltpu.make_async_copy(refs[k], refs[arrays + k], sem.at[k]) for k in range(arrays)]
    for copy in copies:
        copy.start()
    for copy in copies:
        copy.wait()


def per_device(tokens, gain, value_w, output_w, cotangent, base, momentum, delta_values, exps):
    any_place, vmem = pl.BlockSpec(memory_space=pl.ANY), pl.BlockSpec(memory_space=pltpu.VMEM)
    landing = max(sum(cut[m[3]] for m in PLAN) for cut in CUTS)
    shapes = (((1, BLOCK, KV), F32), ((1, BLOCK, KV), F32), ((FRAG, 128), BF16), ((FRAG, 128), F32))
    results = pl.pallas_call(
        kernel,
        out_shape=tuple(pltpu.VMEM(*shape) for shape in shapes),
        in_specs=[any_place, vmem, any_place, any_place, any_place, any_place, any_place, any_place, vmem],
        out_specs=(vmem,) * 4,
        scratch_shapes=[
            pltpu.VMEM((TOK, WIDTH), BF16),
            pltpu.VMEM((TOK, WIDTH), BF16),
            pltpu.VMEM((WIDTH, KV), BF16),
            pltpu.VMEM((WIDTH, KV), BF16),
            pltpu.VMEM((2, TOK, KV), F32),
            pltpu.VMEM((2, TOK, KV), BF16),
            pltpu.VMEM((2, 8, 2 * BLOCK, KV), BF16),
            pltpu.VMEM((2, 8, BLOCK, KV), BF16),
            pltpu.VMEM((2, landing, KV), BF16),
            pltpu.VMEM((FRAG, 128), BF16),
            pltpu.VMEM((3, SEG, 128), BF16),
            pltpu.VMEM((SEG, 128), BF16),
            pltpu.VMEM((SEG, 128), BF16),
            pltpu.VMEM((FRAG, 128), BF16),
            pltpu.SemaphoreType.DMA((MSGS,)),
            pltpu.SemaphoreType.DMA((MSGS,)),
            pltpu.SemaphoreType.DMA((TOK_PARTS + 6,)),
        ],
        compiler_params=pltpu.CompilerParams(
            collective_id=0, has_side_effects=True, vmem_limit_bytes=54 * 2**20
        ),
        name="layer_and_outer_step",
    )(tokens, gain.reshape(1, WIDTH), value_w, output_w, cotangent, base, momentum, delta_values, exps)
    return pl.pallas_call(
        hand_over,
        out_shape=tuple(jax.ShapeDtypeStruct(*shape) for shape in shapes),
        in_specs=[vmem] * 4,
        out_specs=(any_place,) * 4,
        scratch_shapes=[pltpu.SemaphoreType.DMA((4,))],
        compiler_params=pltpu.CompilerParams(vmem_limit_bytes=2**20),
        name="hand_over",
    )(*(pltpu.with_memory_space_constraint(result, pltpu.VMEM) for result in results))


def solution(mesh):
    return jax.shard_map(
        per_device,
        mesh=mesh,
        in_specs=(
            P("replica", "fsdp", None),
            P(),
            P("replica", "fsdp", None),
            P("replica", "fsdp", None),
            P("replica", "fsdp", None),
            P("fsdp", None),
            P("fsdp", None),
            P("replica", "fsdp", None),
            P("replica", "fsdp"),
        ),
        out_specs=(
            P("replica", "fsdp", None),
            P("replica", "fsdp", None),
            P("fsdp", None),
            P("fsdp", None),
        ),
        check_vma=False,
    )
```

```python
import jax
import jax.numpy as jnp
from jax import lax
from jax.experimental import pallas as pl
from jax.experimental.pallas import tpu as pltpu
from jax.sharding import PartitionSpec as P

MESH = pl.DeviceIdType.MESH
F32, BF16 = jnp.float32, jnp.bfloat16
WIDTH, KV, TOK, BLOCK = 4096, 512, 1024, 256
FRAG = 4096
SEG = FRAG // 4
NORM_ROWS = 64
TOK_PARTS = 8
UPDATES = 4

CUTS = ({"A0": 80, "A1": 80, "B0": 48, "B1": 48},) * 2


def plan():
    found = []

    def send(link, block, part, cause):
        dz, dx = block
        lands = {"U": ((dz + 3) % 4, dx), "D": ((dz + 1) % 4, dx), "S": (dz, 1 - dx)}[link]
        found.append((link, block, lands, part, cause))

    for part in ("A0", "A1", "B0", "B1"):
        send("S", (0, 0), part, None)
    for part in ("A0", "B0", "B1", "A1"):
        send("U", (0, 0), part, None)
    for part in ("A1", "B1", "B0", "A0"):
        send("D", (0, 0), part, None)
    k = 0
    while k < len(found):
        link, _, at, part, _ = found[k]
        if at == (0, 1) and part in ("A0", "A1"):
            send("U", at, part, k)
            send("D", at, part, k)
        if at in ((3, 0), (3, 1)) and link == "U" and part in ("A0", "B0"):
            send("U", at, part, k)
        if at in ((1, 0), (1, 1)) and link == "D" and part in ("A1", "B1"):
            send("D", at, part, k)
        if at[1] == 0 and link != "S" and part in ("B0", "B1"):
            send("S", at, part, k)
        k += 1
    return found


PLAN = plan()
CHILDREN = [[c for c, m in enumerate(PLAN) if m[4] == k] for k in range(len(PLAN))]
BLOCKS = [(dz, dx) for dx in (1, 0) for dz in (2, 1, 3, 0)]
COUNT = len(PLAN)
GROUP = COUNT + len(BLOCKS)
DELTA = 4 * GROUP
MSGS = DELTA + 7
BACK = {"U": "D", "D": "U", "S": "S"}
ORDER = (
    ("own", 0, 0), ("own", 0, 4), ("own", 0, 8), ("own", 0, 1), ("own", 0, 5), ("own", 0, 9), ("own", 0, 2),
    ("own", 0, 6), ("own", 0, 10), ("own", 0, 3), ("own", 0, 7), ("own", 0, 11), ("load", 0, 0), ("start", 0, 0),
    ("scale", 0, 0), ("dsend", 0, 0), ("rx", 0, 8), ("norm", 0, 0), ("rx", 0, 5), ("rx", 0, 0), ("rx", 0, 9),
    ("norm", 0, 1), ("rx", 0, 4), ("norm", 0, 2), ("rx", 0, 10), ("rx", 0, 6), ("rx", 0, 1), ("mul", 0, 7),
    ("own", 1, 8), ("own", 1, 9), ("rx", 0, 11), ("own", 1, 4), ("norm", 0, 3), ("rx", 0, 17), ("norm", 0, 4),
    ("rx", 0, 2), ("norm", 0, 5), ("norm", 0, 6), ("own", 1, 0), ("rx", 0, 3), ("norm", 0, 7), ("norm", 0, 8),
    ("norm", 0, 9), ("mul", 0, 5), ("rx", 0, 22), ("own", 1, 5), ("own", 1, 6), ("rx", 0, 21), ("rx", 0, 18),
    ("rx", 0, 20), ("rx", 0, 16), ("rx", 0, 19), ("rx", 0, 23), ("own", 1, 10), ("own", 1, 1), ("own", 1, 2),
    ("rx", 0, 7), ("own", 1, 3), ("norm", 0, 10), ("rx", 0, 26), ("rx", 0, 13), ("norm", 0, 11), ("rx", 0, 15),
    ("norm", 0, 12), ("rx", 0, 12), ("rx", 0, 14), ("own", 1, 11), ("mul", 0, 3), ("own", 1, 7), ("norm", 0, 13),
    ("mul", 0, 4), ("start", 1, 0), ("rx", 1, 4), ("rx", 1, 0), ("rx", 1, 5), ("mul", 0, 6), ("norm", 0, 14),
    ("rx", 1, 10), ("rx", 0, 27), ("rx", 1, 6), ("norm", 0, 15), ("mul", 0, 2), ("mul", 0, 1), ("rx", 1, 9),
    ("rx", 0, 25), ("rx", 0, 24), ("rx", 1, 2), ("rx", 1, 1), ("rx", 1, 8), ("mul", 1, 7), ("rx", 1, 3), ("dsum", 0, 0),
    ("rx", 1, 11), ("mul", 0, 0), ("blk", 0, 0), ("blk", 0, 1), ("rx", 1, 21), ("blk", 0, 2), ("rx", 1, 12),
    ("blk", 0, 3), ("rx", 1, 15), ("rx", 1, 19), ("rx", 1, 23), ("rx", 1, 17), ("blk", 0, 4), ("rx", 1, 7),
    ("rx", 1, 13), ("rx", 1, 22), ("cmb", 0, 0), ("blk", 0, 5), ("rx", 1, 14), ("cmb", 0, 2), ("rx", 1, 18),
    ("cmb", 0, 1), ("blk", 0, 6), ("cmb", 0, 3), ("cmb", 0, 4), ("rx", 1, 16), ("rx", 1, 20), ("mul", 1, 6),
    ("mul", 1, 3), ("dboth", 0, 0), ("snd", 0, 15), ("rx", 1, 27), ("rx", 1, 25), ("cmb", 0, 5), ("snd", 0, 12),
    ("rx", 1, 24), ("rx", 1, 26), ("mul", 1, 1), ("cmb", 0, 6), ("snd", 0, 17), ("mul", 1, 2), ("mul", 1, 4),
    ("snd", 0, 21), ("mul", 1, 5), ("mul", 1, 0), ("blk", 1, 0), ("snd", 0, 8), ("snd", 0, 4), ("blk", 1, 1),
    ("snd", 0, 0), ("snd", 0, 6), ("snd", 0, 10), ("blk", 1, 2), ("cmb", 1, 0), ("snd", 0, 5), ("blk", 1, 3),
    ("blk", 1, 4), ("snd", 0, 9), ("cmb", 1, 1), ("cmb", 1, 2), ("blk", 0, 7), ("blk", 1, 5), ("snd", 1, 15),
    ("snd", 1, 12), ("blk", 1, 6), ("cmb", 1, 3), ("cmb", 1, 4), ("blk", 1, 7), ("snd", 1, 17), ("snd", 0, 1),
    ("snd", 1, 21), ("cmb", 1, 5), ("cmb", 1, 6), ("snd", 1, 1), ("snd", 1, 0), ("snd", 1, 10), ("snd", 1, 6),
    ("cmb", 1, 7), ("upd", 0, 0), ("upd", 0, 1), ("cmb", 0, 7), ("snd", 1, 8), ("snd", 1, 4), ("snd", 1, 9),
    ("upd", 0, 2), ("fin", 0, 2), ("snd", 1, 5), ("fin", 0, 1), ("fin", 0, 0), ("fin", 1, 1), ("fin", 0, 3),
    ("upd", 0, 3), ("fin", 1, 0), ("fin", 1, 3), ("fin", 1, 2),
)


def kernel(
    tok_in,
    gain,
    wv_in,
    wo_in,
    cot_in,
    base_in,
    mom_in,
    dv_in,
    exps,
    vg_out,
    og_out,
    base,
    mom,
    normed,
    cot,
    wv,
    wo,
    acc,
    factors,
    partial,
    from_core,
    landed,
    scaled,
    segs,
    seg_own,
    seg_x,
    delta,
    send_sem,
    recv_sem,
    load_sem,
    ready_sem,
):
    r, f = lax.axis_index("replica"), lax.axis_index("fsdp")
    x_lo, y = r // 4, lax.rem(r, 4)
    z, x, c = f // 4, lax.rem(f // 2, 2), lax.rem(f, 2)

    def chip(block):
        dz, dx = block
        return lax.rem(z + dz, 4) * 2 + (1 - x if dx else x)

    to_core = {"fsdp": chip((0, 0)) * 2 + 1 - c}
    to = {"U": {"fsdp": chip((1, 0)) * 2 + c}, "D": {"fsdp": chip((3, 0)) * 2 + c}, "S": {"fsdp": chip((0, 1)) * 2 + c}}
    to_y = [{"replica": x_lo * 4 + lax.rem(y + k, 4)} for k in (1, 2, 3)]
    to_side = {"replica": (1 - x_lo) * 4 + y}

    sent = []

    def copy_of(k, src, dst, device):
        return pltpu.make_async_remote_copy(
            src_ref=src,
            dst_ref=dst,
            send_sem=send_sem.at[k],
            recv_sem=recv_sem.at[k],
            device_id=device,
            device_id_type=MESH,
        )

    def send(k, src, dst, device):
        sent.append(copy_of(k, src, dst, device))
        sent[-1].start()

    def arrive(k, dst):
        copy_of(k, dst, dst, to_core).wait_recv()

    loads, waited = {}, set()

    def load(name, src, dst):
        loads[name] = pltpu.make_async_copy(src, dst, load_sem.at[len(loads)])
        loads[name].start()

    def loaded(name):
        if name not in waited:
            waited.add(name)
            loads[name].wait()

    weights, weights_in = (wo, wv), (wo_in, wv_in)
    left, right, outs = (cot, normed), (normed, cot), (vg_out, og_out)

    def rows_of(g, part):
        cut = CUTS[g]
        first = 0
        for name in ("A0", "A1", "B0", "B1"):
            if name == part:
                return first, cut[name]
            first += cut[name]
        return 0, BLOCK

    def weight(g, block, core, part=None):
        first, count = rows_of(g, part)
        return weights[g].at[pl.ds(pl.multiple_of((chip(block) * 2 + core) * BLOCK + first, 16), count)]

    barrier = pltpu.get_barrier_semaphore()
    for device in (to["S"], to["U"], to["D"], to_core):
        pl.semaphore_signal(barrier, inc=1, device_id=device, device_id_type=MESH)

    def greet(sem, towards_higher):
        for k in (1, 2, 3):

            @pl.when((y + k < 4) if towards_higher else (y + k >= 4))
            def _():
                pl.semaphore_signal(sem, inc=1, device_id=to_y[k - 1], device_id_type=MESH)

        @pl.when(x_lo == (0 if towards_higher else 1))
        def _():
            pl.semaphore_signal(sem, inc=1, device_id=to_side, device_id_type=MESH)

    greet(barrier, True)
    pl.semaphore_wait(barrier, 4 + y + x_lo)

    load("own0", wo_in.at[0], weight(0, (0, 0), c))
    load("own1", wv_in.at[0], weight(1, (0, 0), c))

    def load_rest(_, __):
        greet(ready_sem, False)
        load("dv", dv_in.at[0], scaled)
        load("cot", cot_in.at[0], cot)
        for k in range(TOK_PARTS):
            rows = pl.ds(k * (TOK // TOK_PARTS), TOK // TOK_PARTS)
            load(("tok", k), tok_in.at[0, rows], normed.at[rows])
        load("base", base_in, base)
        load("mom", mom_in, mom)

    received = {}
    multiplied = [0, 0]

    def start(g, _):
        send(g * GROUP + COUNT + BLOCKS.index((0, 0)), weights_in[g].at[0], weight(g, (0, 0), c), to_core)

    def own(g, k):
        first, count = rows_of(g, PLAN[k][3])
        piece = weights_in[g].at[0, pl.ds(first, count)]
        send(g * GROUP + k, piece, weight(g, (0, 0), c, PLAN[k][3]), to[PLAN[k][0]])

    def rx(g, k):
        _, _, block, part, _ = PLAN[k]
        piece = weight(g, block, c, part)
        arrive(g * GROUP + k, piece)
        for child in CHILDREN[k]:
            send(g * GROUP + child, piece, piece, to[PLAN[child][0]])
        received[g, block] = received.get((g, block), 0) + 1
        if received[g, block] == 4:
            whole = weight(g, block, c)
            send(g * GROUP + COUNT + BLOCKS.index(block), whole, whole, to_core)

    def mul(g, b):
        block = BLOCKS[b]
        if block == (0, 0):
            loaded("own%d" % g)
        if g == 0:
            loaded("cot")
        arrive(g * GROUP + COUNT + b, weight(g, block, 1 - c))
        both = pl.ds(pl.multiple_of(chip(block) * 2 * BLOCK, 2 * BLOCK), 2 * BLOCK)
        term = jnp.dot(left[g][:, both], weights[g][both, :], preferred_element_type=F32)
        multiplied[g] += 1
        if multiplied[g] == 1:
            acc[g] = term
        elif multiplied[g] < len(BLOCKS):
            acc[g] += term
        else:
            factors[g] = (acc[g] + term).astype(BF16)

    def mine(g, b, part=None):
        first, count = rows_of(g, part)
        return partial.at[g, b, pl.ds(pl.multiple_of(c * BLOCK + first, 16), count)]

    def slot(g, k):
        first = sum(CUTS[g][m[3]] for m in PLAN[:k])
        return landed.at[g, pl.ds(first, CUTS[g][PLAN[k][3]])]

    def add(ref, term):
        ref[...] = (ref[...].astype(F32) + term[...].astype(F32)).astype(BF16)

    def blk(g, b):
        columns = pl.ds(pl.multiple_of(chip(BLOCKS[b]) * 2 * BLOCK, 2 * BLOCK), 2 * BLOCK)
        term = lax.dot_general(right[g][:, columns], factors[g], (((0,), (0,)), ((), ())), preferred_element_type=F32)
        partial[g, b] = term.astype(BF16)
        theirs = partial.at[g, b, pl.ds(pl.multiple_of((1 - c) * BLOCK, BLOCK), BLOCK)]
        send((2 + g) * GROUP + COUNT + b, theirs, from_core.at[g, b], to_core)

    def ship(g, k):
        link, _, block, part, _ = PLAN[k]
        send((2 + g) * GROUP + k, mine(g, BLOCKS.index(block), part), slot(g, k), to[BACK[link]])

    def cmb(g, b):
        arrive((2 + g) * GROUP + COUNT + b, from_core.at[g, b])
        add(mine(g, b), from_core.at[g, b])
        for k, m in enumerate(PLAN):
            if m[2] == BLOCKS[b] and not CHILDREN[k]:
                ship(g, k)

    def snd(g, k):
        piece = mine(g, BLOCKS.index(PLAN[k][2]), PLAN[k][3])
        for child in CHILDREN[k]:
            arrive((2 + g) * GROUP + child, slot(g, child))
            add(piece, slot(g, child))
        ship(g, k)

    def fin(g, i):
        part = ("A0", "A1", "B0", "B1")[i]
        first, count = rows_of(g, part)
        total = mine(g, BLOCKS.index((0, 0)), part)[...].astype(F32)
        for k, m in enumerate(PLAN):
            if m[4] is None and m[3] == part:
                arrive((2 + g) * GROUP + k, slot(g, k))
                total += slot(g, k)[...].astype(F32)
        outs[g][0, pl.ds(first, count), :] = total

    def norm(_, i):
        loaded(("tok", i * NORM_ROWS // (TOK // TOK_PARTS)))
        at = pl.ds(i * NORM_ROWS, NORM_ROWS)
        value = normed[at, :].astype(F32)
        scale = lax.rsqrt(jnp.mean(value * value, axis=1, keepdims=True) + 1e-05)
        normed[at, :] = (value * scale * gain[...]).astype(BF16)

    def seg(buf, k):
        return buf.at[pl.ds(pl.multiple_of(lax.rem(y + k, 4) * SEG, SEG), SEG)]

    def scale(_, __):
        loaded("dv")

        def some(m, _):
            at = pl.ds(pl.multiple_of(m * 128, 128), 128)
            factor = jnp.exp2(exps[:, at].astype(F32))
            factor = jnp.broadcast_to(factor, (128, 128)).T
            scaled[at, :] = (scaled[at, :].astype(F32) * factor).astype(BF16)
            return 0

        lax.fori_loop(0, FRAG // 128, some, 0, unroll=4)

    def dsend(_, __):
        higher = 4 - y - x_lo

        @pl.when(higher > 0)
        def _():
            pl.semaphore_wait(ready_sem, higher)

        for k in (1, 2, 3):
            send(DELTA + k - 1, seg(scaled, k), segs.at[k - 1], to_y[k - 1])

    def dsum(_, __):
        for k in (1, 2, 3):
            arrive(DELTA + k - 1, segs.at[k - 1])

        def some(m, _):
            at = pl.ds(pl.multiple_of(m * 128, 128), 128)
            value = scaled[pl.ds(pl.multiple_of(y * SEG + m * 128, 128), 128), :].astype(F32)
            for k in range(3):
                value += segs[k, at, :].astype(F32)
            seg_own[at, :] = value.astype(BF16)
            return 0

        lax.fori_loop(0, SEG // 128, some, 0)
        send(DELTA + 3, seg_own, seg_x, to_side)

    def dboth(_, __):
        arrive(DELTA + 3, seg_x)

        def some(m, _):
            at = pl.ds(pl.multiple_of(m * 128, 128), 128)
            value = seg_own[at, :].astype(F32) + seg_x[at, :].astype(F32)
            delta[pl.ds(pl.multiple_of(y * SEG + m * 128, 128), 128), :] = value.astype(BF16)
            return 0

        lax.fori_loop(0, SEG // 128, some, 0)
        for k in (1, 2, 3):
            send(DELTA + 3 + k, seg(delta, 0), seg(delta, 0), to_y[k - 1])

    def upd(_, i):
        if i == 0:
            for k in (1, 2, 3):
                arrive(DELTA + 3 + k, seg(delta, 4 - k))
            loaded("base")
            loaded("mom")

        def some(m, _):
            at = pl.ds(pl.multiple_of(i * (FRAG // UPDATES) + m * 128, 128), 128)
            mean = delta[at, :].astype(F32) * 0.125
            new = 0.9 * mom[at, :] + mean
            mom[at, :] = new
            base[at, :] = (base[at, :].astype(F32) - 0.7 * (mean + 0.9 * new)).astype(BF16)
            return 0

        lax.fori_loop(0, FRAG // UPDATES // 128, some, 0)

    tasks = {
        "start": start,
        "own": own,
        "load": load_rest,
        "rx": rx,
        "mul": mul,
        "blk": blk,
        "cmb": cmb,
        "snd": snd,
        "fin": fin,
        "norm": norm,
        "scale": scale,
        "dsend": dsend,
        "dsum": dsum,
        "dboth": dboth,
        "upd": upd,
    }
    for name, g, k in ORDER:
        tasks[name](g, k)
    for copy in sent:
        copy.wait_send()


def hand_over(*refs):
    sem = refs[-1]
    arrays = (len(refs) - 1) // 2
    copies = [pltpu.make_async_copy(refs[k], refs[arrays + k], sem.at[k]) for k in range(arrays)]
    for copy in copies:
        copy.start()
    for copy in copies:
        copy.wait()


def per_device(tokens, gain, value_w, output_w, cotangent, base, momentum, delta_values, exps):
    any_place, vmem = pl.BlockSpec(memory_space=pl.ANY), pl.BlockSpec(memory_space=pltpu.VMEM)
    landing = max(sum(cut[m[3]] for m in PLAN) for cut in CUTS)
    shapes = (((1, BLOCK, KV), F32), ((1, BLOCK, KV), F32), ((FRAG, 128), BF16), ((FRAG, 128), F32))
    results = pl.pallas_call(
        kernel,
        out_shape=tuple(pltpu.VMEM(*shape) for shape in shapes),
        in_specs=[any_place, vmem, any_place, any_place, any_place, any_place, any_place, any_place, vmem],
        out_specs=(vmem,) * 4,
        scratch_shapes=[
            pltpu.VMEM((TOK, WIDTH), BF16),
            pltpu.VMEM((TOK, WIDTH), BF16),
            pltpu.VMEM((WIDTH, KV), BF16),
            pltpu.VMEM((WIDTH, KV), BF16),
            pltpu.VMEM((2, TOK, KV), F32),
            pltpu.VMEM((2, TOK, KV), BF16),
            pltpu.VMEM((2, 8, 2 * BLOCK, KV), BF16),
            pltpu.VMEM((2, 8, BLOCK, KV), BF16),
            pltpu.VMEM((2, landing, KV), BF16),
            pltpu.VMEM((FRAG, 128), BF16),
            pltpu.VMEM((3, SEG, 128), BF16),
            pltpu.VMEM((SEG, 128), BF16),
            pltpu.VMEM((SEG, 128), BF16),
            pltpu.VMEM((FRAG, 128), BF16),
            pltpu.SemaphoreType.DMA((MSGS,)),
            pltpu.SemaphoreType.DMA((MSGS,)),
            pltpu.SemaphoreType.DMA((TOK_PARTS + 6,)),
            pltpu.SemaphoreType.REGULAR,
        ],
        compiler_params=pltpu.CompilerParams(
            collective_id=0, has_side_effects=True, vmem_limit_bytes=54 * 2**20
        ),
        name="layer_and_outer_step",
    )(tokens, gain.reshape(1, WIDTH), value_w, output_w, cotangent, base, momentum, delta_values, exps)
    return pl.pallas_call(
        hand_over,
        out_shape=tuple(jax.ShapeDtypeStruct(*shape) for shape in shapes),
        in_specs=[vmem] * 4,
        out_specs=(any_place,) * 4,
        scratch_shapes=[pltpu.SemaphoreType.DMA((4,))],
        compiler_params=pltpu.CompilerParams(vmem_limit_bytes=2**20),
        name="hand_over",
    )(*(pltpu.with_memory_space_constraint(result, pltpu.VMEM) for result in results))


def solution(mesh):
    return jax.shard_map(
        per_device,
        mesh=mesh,
        in_specs=(
            P("replica", "fsdp", None),
            P(),
            P("replica", "fsdp", None),
            P("replica", "fsdp", None),
            P("replica", "fsdp", None),
            P("fsdp", None),
            P("fsdp", None),
            P("replica", "fsdp", None),
            P("replica", "fsdp"),
        ),
        out_specs=(
            P("replica", "fsdp", None),
            P("replica", "fsdp", None),
            P("fsdp", None),
            P("fsdp", None),
        ),
        check_vma=False,
    )
```

```python
import jax
import jax.numpy as jnp
from jax import lax
from jax.experimental import pallas as pl
from jax.experimental.pallas import tpu as pltpu
from jax.sharding import PartitionSpec as P

MESH = pl.DeviceIdType.MESH
F32, BF16 = jnp.float32, jnp.bfloat16
WIDTH, KV, TOK, BLOCK = 4096, 512, 1024, 256
FRAG = 4096
SEG = FRAG // 4
NORM_ROWS = 64
TOK_PARTS = 8
UPDATES = 4

CUTS = ({"A0": 80, "A1": 80, "B0": 48, "B1": 48},) * 2


def plan():
    found = []

    def send(link, block, part, cause):
        dz, dx = block
        lands = {"U": ((dz + 3) % 4, dx), "D": ((dz + 1) % 4, dx), "S": (dz, 1 - dx)}[link]
        found.append((link, block, lands, part, cause))

    for part in ("A0", "A1", "B0", "B1"):
        send("S", (0, 0), part, None)
    for part in ("A0", "B0", "B1", "A1"):
        send("U", (0, 0), part, None)
    for part in ("A1", "B1", "B0", "A0"):
        send("D", (0, 0), part, None)
    k = 0
    while k < len(found):
        link, _, at, part, _ = found[k]
        if at == (0, 1) and part in ("A0", "A1"):
            send("U", at, part, k)
            send("D", at, part, k)
        if at in ((3, 0), (3, 1)) and link == "U" and part in ("A0", "B0"):
            send("U", at, part, k)
        if at in ((1, 0), (1, 1)) and link == "D" and part in ("A1", "B1"):
            send("D", at, part, k)
        if at[1] == 0 and link != "S" and part in ("B0", "B1"):
            send("S", at, part, k)
        k += 1
    return found


PLAN = plan()
CHILDREN = [[c for c, m in enumerate(PLAN) if m[4] == k] for k in range(len(PLAN))]
BLOCKS = [(dz, dx) for dx in (1, 0) for dz in (2, 1, 3, 0)]
COUNT = len(PLAN)
GROUP = COUNT + len(BLOCKS)
DELTA = 4 * GROUP
MSGS = DELTA + 7
BACK = {"U": "D", "D": "U", "S": "S"}
ORDER = (
    ("own", 0, 0), ("own", 0, 4), ("own", 0, 8), ("own", 0, 1), ("own", 0, 5), ("own", 0, 9), ("own", 0, 2),
    ("own", 0, 6), ("own", 0, 10), ("own", 0, 3), ("own", 0, 7), ("own", 0, 11), ("load", 0, 0), ("start", 0, 0),
    ("scale", 0, 0), ("dsend", 0, 0), ("rx", 0, 8), ("norm", 0, 0), ("rx", 0, 5), ("rx", 0, 0), ("rx", 0, 9),
    ("norm", 0, 1), ("rx", 0, 4), ("norm", 0, 2), ("rx", 0, 10), ("rx", 0, 6), ("rx", 0, 1), ("mul", 0, 7),
    ("own", 1, 8), ("own", 1, 9), ("rx", 0, 11), ("own", 1, 4), ("norm", 0, 3), ("rx", 0, 17), ("norm", 0, 4),
    ("rx", 0, 2), ("norm", 0, 5), ("norm", 0, 6), ("own", 1, 0), ("rx", 0, 3), ("norm", 0, 7), ("norm", 0, 8),
    ("norm", 0, 9), ("mul", 0, 5), ("rx", 0, 22), ("own", 1, 5), ("own", 1, 6), ("rx", 0, 21), ("rx", 0, 18),
    ("rx", 0, 20), ("rx", 0, 16), ("rx", 0, 19), ("rx", 0, 23), ("own", 1, 10), ("own", 1, 1), ("own", 1, 2),
    ("rx", 0, 7), ("own", 1, 3), ("norm", 0, 10), ("rx", 0, 26), ("rx", 0, 13), ("norm", 0, 11), ("rx", 0, 15),
    ("norm", 0, 12), ("rx", 0, 12), ("rx", 0, 14), ("own", 1, 11), ("mul", 0, 3), ("own", 1, 7), ("norm", 0, 13),
    ("mul", 0, 4), ("start", 1, 0), ("rx", 1, 4), ("rx", 1, 0), ("rx", 1, 5), ("mul", 0, 6), ("norm", 0, 14),
    ("rx", 1, 10), ("rx", 0, 27), ("rx", 1, 6), ("norm", 0, 15), ("mul", 0, 2), ("mul", 0, 1), ("rx", 1, 9),
    ("rx", 0, 25), ("rx", 0, 24), ("rx", 1, 2), ("rx", 1, 1), ("rx", 1, 8), ("mul", 1, 7), ("rx", 1, 3), ("dsum", 0, 0),
    ("rx", 1, 11), ("mul", 0, 0), ("blk", 0, 0), ("blk", 0, 1), ("rx", 1, 21), ("blk", 0, 2), ("rx", 1, 12),
    ("blk", 0, 3), ("rx", 1, 15), ("rx", 1, 19), ("rx", 1, 23), ("rx", 1, 17), ("blk", 0, 4), ("rx", 1, 7),
    ("rx", 1, 13), ("rx", 1, 22), ("cmb", 0, 0), ("blk", 0, 5), ("rx", 1, 14), ("cmb", 0, 2), ("rx", 1, 18),
    ("cmb", 0, 1), ("blk", 0, 6), ("cmb", 0, 3), ("cmb", 0, 4), ("rx", 1, 16), ("rx", 1, 20), ("mul", 1, 6),
    ("mul", 1, 3), ("dboth", 0, 0), ("snd", 0, 15), ("rx", 1, 27), ("rx", 1, 25), ("cmb", 0, 5), ("snd", 0, 12),
    ("rx", 1, 24), ("rx", 1, 26), ("mul", 1, 1), ("cmb", 0, 6), ("snd", 0, 17), ("mul", 1, 2), ("mul", 1, 4),
    ("snd", 0, 21), ("mul", 1, 5), ("mul", 1, 0), ("blk", 1, 0), ("snd", 0, 8), ("snd", 0, 4), ("blk", 1, 1),
    ("snd", 0, 0), ("snd", 0, 6), ("snd", 0, 10), ("blk", 1, 2), ("cmb", 1, 0), ("snd", 0, 5), ("blk", 1, 3),
    ("blk", 1, 4), ("snd", 0, 9), ("cmb", 1, 1), ("cmb", 1, 2), ("blk", 0, 7), ("blk", 1, 5), ("snd", 1, 15),
    ("snd", 1, 12), ("blk", 1, 6), ("cmb", 1, 3), ("cmb", 1, 4), ("blk", 1, 7), ("snd", 1, 17), ("snd", 0, 1),
    ("snd", 1, 21), ("cmb", 1, 5), ("cmb", 1, 6), ("snd", 1, 1), ("snd", 1, 0), ("snd", 1, 10), ("snd", 1, 6),
    ("cmb", 1, 7), ("upd", 0, 0), ("upd", 0, 1), ("cmb", 0, 7), ("snd", 1, 8), ("snd", 1, 4), ("snd", 1, 9),
    ("upd", 0, 2), ("fin", 0, 2), ("snd", 1, 5), ("fin", 0, 1), ("fin", 0, 0), ("fin", 1, 1), ("fin", 0, 3),
    ("upd", 0, 3), ("fin", 1, 0), ("fin", 1, 3), ("fin", 1, 2),
)


def kernel(
    tok_in,
    gain,
    wv_in,
    wo_in,
    cot_in,
    base_in,
    mom_in,
    dv_in,
    exps,
    vg_out,
    og_out,
    base,
    mom,
    normed,
    cot,
    wv,
    wo,
    acc,
    factors,
    partial,
    from_core,
    landed,
    scaled,
    segs,
    seg_own,
    seg_x,
    delta,
    send_sem,
    recv_sem,
    load_sem,
    ready_sem,
):
    r, f = lax.axis_index("replica"), lax.axis_index("fsdp")
    x_lo, y = r // 4, lax.rem(r, 4)
    z, x, c = f // 4, lax.rem(f // 2, 2), lax.rem(f, 2)

    def chip(block):
        dz, dx = block
        return lax.rem(z + dz, 4) * 2 + (1 - x if dx else x)

    to_core = {"fsdp": chip((0, 0)) * 2 + 1 - c}
    to = {"U": {"fsdp": chip((1, 0)) * 2 + c}, "D": {"fsdp": chip((3, 0)) * 2 + c}, "S": {"fsdp": chip((0, 1)) * 2 + c}}
    to_y = [{"replica": x_lo * 4 + lax.rem(y + k, 4)} for k in (1, 2, 3)]
    to_side = {"replica": (1 - x_lo) * 4 + y}

    sent = []

    def copy_of(k, src, dst, device):
        return pltpu.make_async_remote_copy(
            src_ref=src,
            dst_ref=dst,
            send_sem=send_sem.at[k],
            recv_sem=recv_sem.at[k],
            device_id=device,
            device_id_type=MESH,
        )

    def send(k, src, dst, device):
        sent.append(copy_of(k, src, dst, device))
        sent[-1].start()

    def arrive(k, dst):
        copy_of(k, dst, dst, to_core).wait_recv()

    loads, waited = {}, set()

    def load(name, src, dst):
        loads[name] = pltpu.make_async_copy(src, dst, load_sem.at[len(loads)])
        loads[name].start()

    def loaded(name):
        if name not in waited:
            waited.add(name)
            loads[name].wait()

    weights, weights_in = (wo, wv), (wo_in, wv_in)
    left, right, outs = (cot, normed), (normed, cot), (vg_out, og_out)

    def rows_of(g, part):
        cut = CUTS[g]
        first = 0
        for name in ("A0", "A1", "B0", "B1"):
            if name == part:
                return first, cut[name]
            first += cut[name]
        return 0, BLOCK

    def weight(g, block, core, part=None):
        first, count = rows_of(g, part)
        return weights[g].at[pl.ds(pl.multiple_of((chip(block) * 2 + core) * BLOCK + first, 16), count)]

    barrier = pltpu.get_barrier_semaphore()
    for device in (to["S"], to["U"], to["D"], to_core):
        pl.semaphore_signal(barrier, inc=1, device_id=device, device_id_type=MESH)

    def greet(sem, towards_higher):
        for k in (1, 2, 3):

            @pl.when((y + k < 4) if towards_higher else (y + k >= 4))
            def _():
                pl.semaphore_signal(sem, inc=1, device_id=to_y[k - 1], device_id_type=MESH)

        @pl.when(x_lo == (0 if towards_higher else 1))
        def _():
            pl.semaphore_signal(sem, inc=1, device_id=to_side, device_id_type=MESH)

    greet(barrier, True)
    pl.semaphore_wait(barrier, 4 + y + x_lo)


    def load_rest(_, __):
        load("own0", wo_in.at[0], weight(0, (0, 0), c))
        load("own1", wv_in.at[0], weight(1, (0, 0), c))
        greet(ready_sem, False)
        load("dv", dv_in.at[0], scaled)
        load("cot", cot_in.at[0], cot)
        for k in range(TOK_PARTS):
            rows = pl.ds(k * (TOK // TOK_PARTS), TOK // TOK_PARTS)
            load(("tok", k), tok_in.at[0, rows], normed.at[rows])
        load("base", base_in, base)
        load("mom", mom_in, mom)

    received = {}
    multiplied = [0, 0]

    def start(g, _):
        send(g * GROUP + COUNT + BLOCKS.index((0, 0)), weights_in[g].at[0], weight(g, (0, 0), c), to_core)

    def own(g, k):
        first, count = rows_of(g, PLAN[k][3])
        piece = weights_in[g].at[0, pl.ds(first, count)]
        send(g * GROUP + k, piece, weight(g, (0, 0), c, PLAN[k][3]), to[PLAN[k][0]])

    def rx(g, k):
        _, _, block, part, _ = PLAN[k]
        piece = weight(g, block, c, part)
        arrive(g * GROUP + k, piece)
        for child in CHILDREN[k]:
            send(g * GROUP + child, piece, piece, to[PLAN[child][0]])
        received[g, block] = received.get((g, block), 0) + 1
        if received[g, block] == 4:
            whole = weight(g, block, c)
            send(g * GROUP + COUNT + BLOCKS.index(block), whole, whole, to_core)

    def mul(g, b):
        block = BLOCKS[b]
        if block == (0, 0):
            loaded("own%d" % g)
        if g == 0:
            loaded("cot")
        arrive(g * GROUP + COUNT + b, weight(g, block, 1 - c))
        both = pl.ds(pl.multiple_of(chip(block) * 2 * BLOCK, 2 * BLOCK), 2 * BLOCK)
        term = jnp.dot(left[g][:, both], weights[g][both, :], preferred_element_type=F32)
        multiplied[g] += 1
        if multiplied[g] == 1:
            acc[g] = term
        elif multiplied[g] < len(BLOCKS):
            acc[g] += term
        else:
            factors[g] = (acc[g] + term).astype(BF16)

    def mine(g, b, part=None):
        first, count = rows_of(g, part)
        return partial.at[g, b, pl.ds(pl.multiple_of(c * BLOCK + first, 16), count)]

    def slot(g, k):
        first = sum(CUTS[g][m[3]] for m in PLAN[:k])
        return landed.at[g, pl.ds(first, CUTS[g][PLAN[k][3]])]

    def add(ref, term):
        ref[...] = (ref[...].astype(F32) + term[...].astype(F32)).astype(BF16)

    def blk(g, b):
        columns = pl.ds(pl.multiple_of(chip(BLOCKS[b]) * 2 * BLOCK, 2 * BLOCK), 2 * BLOCK)
        term = lax.dot_general(right[g][:, columns], factors[g], (((0,), (0,)), ((), ())), preferred_element_type=F32)
        partial[g, b] = term.astype(BF16)
        theirs = partial.at[g, b, pl.ds(pl.multiple_of((1 - c) * BLOCK, BLOCK), BLOCK)]
        send((2 + g) * GROUP + COUNT + b, theirs, from_core.at[g, b], to_core)

    def ship(g, k):
        link, _, block, part, _ = PLAN[k]
        send((2 + g) * GROUP + k, mine(g, BLOCKS.index(block), part), slot(g, k), to[BACK[link]])

    def cmb(g, b):
        arrive((2 + g) * GROUP + COUNT + b, from_core.at[g, b])
        add(mine(g, b), from_core.at[g, b])
        for k, m in enumerate(PLAN):
            if m[2] == BLOCKS[b] and not CHILDREN[k]:
                ship(g, k)

    def snd(g, k):
        piece = mine(g, BLOCKS.index(PLAN[k][2]), PLAN[k][3])
        for child in CHILDREN[k]:
            arrive((2 + g) * GROUP + child, slot(g, child))
            add(piece, slot(g, child))
        ship(g, k)

    def fin(g, i):
        part = ("A0", "A1", "B0", "B1")[i]
        first, count = rows_of(g, part)
        total = mine(g, BLOCKS.index((0, 0)), part)[...].astype(F32)
        for k, m in enumerate(PLAN):
            if m[4] is None and m[3] == part:
                arrive((2 + g) * GROUP + k, slot(g, k))
                total += slot(g, k)[...].astype(F32)
        outs[g][0, pl.ds(first, count), :] = total

    def norm(_, i):
        loaded(("tok", i * NORM_ROWS // (TOK // TOK_PARTS)))
        at = pl.ds(i * NORM_ROWS, NORM_ROWS)
        value = normed[at, :].astype(F32)
        scale = lax.rsqrt(jnp.mean(value * value, axis=1, keepdims=True) + 1e-05)
        normed[at, :] = (value * scale * gain[...]).astype(BF16)

    def seg(buf, k):
        return buf.at[pl.ds(pl.multiple_of(lax.rem(y + k, 4) * SEG, SEG), SEG)]

    def scale(_, __):
        loaded("dv")

        def some(m, _):
            at = pl.ds(pl.multiple_of(m * 128, 128), 128)
            factor = jnp.exp2(exps[:, at].astype(F32))
            factor = jnp.broadcast_to(factor, (128, 128)).T
            scaled[at, :] = (scaled[at, :].astype(F32) * factor).astype(BF16)
            return 0

        lax.fori_loop(0, FRAG // 128, some, 0, unroll=4)

    def dsend(_, __):
        higher = 4 - y - x_lo

        @pl.when(higher > 0)
        def _():
            pl.semaphore_wait(ready_sem, higher)

        for k in (1, 2, 3):
            send(DELTA + k - 1, seg(scaled, k), segs.at[k - 1], to_y[k - 1])

    def dsum(_, __):
        for k in (1, 2, 3):
            arrive(DELTA + k - 1, segs.at[k - 1])

        def some(m, _):
            at = pl.ds(pl.multiple_of(m * 128, 128), 128)
            value = scaled[pl.ds(pl.multiple_of(y * SEG + m * 128, 128), 128), :].astype(F32)
            for k in range(3):
                value += segs[k, at, :].astype(F32)
            seg_own[at, :] = value.astype(BF16)
            return 0

        lax.fori_loop(0, SEG // 128, some, 0)
        send(DELTA + 3, seg_own, seg_x, to_side)

    def dboth(_, __):
        arrive(DELTA + 3, seg_x)

        def some(m, _):
            at = pl.ds(pl.multiple_of(m * 128, 128), 128)
            value = seg_own[at, :].astype(F32) + seg_x[at, :].astype(F32)
            delta[pl.ds(pl.multiple_of(y * SEG + m * 128, 128), 128), :] = value.astype(BF16)
            return 0

        lax.fori_loop(0, SEG // 128, some, 0)
        for k in (1, 2, 3):
            send(DELTA + 3 + k, seg(delta, 0), seg(delta, 0), to_y[k - 1])

    def upd(_, i):
        if i == 0:
            for k in (1, 2, 3):
                arrive(DELTA + 3 + k, seg(delta, 4 - k))
            loaded("base")
            loaded("mom")

        def some(m, _):
            at = pl.ds(pl.multiple_of(i * (FRAG // UPDATES) + m * 128, 128), 128)
            mean = delta[at, :].astype(F32) * 0.125
            new = 0.9 * mom[at, :] + mean
            mom[at, :] = new
            base[at, :] = (base[at, :].astype(F32) - 0.7 * (mean + 0.9 * new)).astype(BF16)
            return 0

        lax.fori_loop(0, FRAG // UPDATES // 128, some, 0)

    tasks = {
        "start": start,
        "own": own,
        "load": load_rest,
        "rx": rx,
        "mul": mul,
        "blk": blk,
        "cmb": cmb,
        "snd": snd,
        "fin": fin,
        "norm": norm,
        "scale": scale,
        "dsend": dsend,
        "dsum": dsum,
        "dboth": dboth,
        "upd": upd,
    }
    for name, g, k in ORDER:
        tasks[name](g, k)
    for copy in sent:
        copy.wait_send()


def hand_over(*refs):
    sem = refs[-1]
    arrays = (len(refs) - 1) // 2
    copies = [pltpu.make_async_copy(refs[k], refs[arrays + k], sem.at[k]) for k in range(arrays)]
    for copy in copies:
        copy.start()
    for copy in copies:
        copy.wait()


def per_device(tokens, gain, value_w, output_w, cotangent, base, momentum, delta_values, exps):
    any_place, vmem = pl.BlockSpec(memory_space=pl.ANY), pl.BlockSpec(memory_space=pltpu.VMEM)
    landing = max(sum(cut[m[3]] for m in PLAN) for cut in CUTS)
    shapes = (((1, BLOCK, KV), F32), ((1, BLOCK, KV), F32), ((FRAG, 128), BF16), ((FRAG, 128), F32))
    results = pl.pallas_call(
        kernel,
        out_shape=tuple(pltpu.VMEM(*shape) for shape in shapes),
        in_specs=[any_place, vmem, any_place, any_place, any_place, any_place, any_place, any_place, vmem],
        out_specs=(vmem,) * 4,
        scratch_shapes=[
            pltpu.VMEM((TOK, WIDTH), BF16),
            pltpu.VMEM((TOK, WIDTH), BF16),
            pltpu.VMEM((WIDTH, KV), BF16),
            pltpu.VMEM((WIDTH, KV), BF16),
            pltpu.VMEM((2, TOK, KV), F32),
            pltpu.VMEM((2, TOK, KV), BF16),
            pltpu.VMEM((2, 8, 2 * BLOCK, KV), BF16),
            pltpu.VMEM((2, 8, BLOCK, KV), BF16),
            pltpu.VMEM((2, landing, KV), BF16),
            pltpu.VMEM((FRAG, 128), BF16),
            pltpu.VMEM((3, SEG, 128), BF16),
            pltpu.VMEM((SEG, 128), BF16),
            pltpu.VMEM((SEG, 128), BF16),
            pltpu.VMEM((FRAG, 128), BF16),
            pltpu.SemaphoreType.DMA((MSGS,)),
            pltpu.SemaphoreType.DMA((MSGS,)),
            pltpu.SemaphoreType.DMA((TOK_PARTS + 6,)),
            pltpu.SemaphoreType.REGULAR,
        ],
        compiler_params=pltpu.CompilerParams(
            collective_id=0, has_side_effects=True, vmem_limit_bytes=54 * 2**20
        ),
        name="layer_and_outer_step",
    )(tokens, gain.reshape(1, WIDTH), value_w, output_w, cotangent, base, momentum, delta_values, exps)
    return pl.pallas_call(
        hand_over,
        out_shape=tuple(jax.ShapeDtypeStruct(*shape) for shape in shapes),
        in_specs=[vmem] * 4,
        out_specs=(any_place,) * 4,
        scratch_shapes=[pltpu.SemaphoreType.DMA((4,))],
        compiler_params=pltpu.CompilerParams(vmem_limit_bytes=2**20),
        name="hand_over",
    )(*(pltpu.with_memory_space_constraint(result, pltpu.VMEM) for result in results))


def solution(mesh):
    return jax.shard_map(
        per_device,
        mesh=mesh,
        in_specs=(
            P("replica", "fsdp", None),
            P(),
            P("replica", "fsdp", None),
            P("replica", "fsdp", None),
            P("replica", "fsdp", None),
            P("fsdp", None),
            P("fsdp", None),
            P("replica", "fsdp", None),
            P("replica", "fsdp"),
        ),
        out_specs=(
            P("replica", "fsdp", None),
            P("replica", "fsdp", None),
            P("fsdp", None),
            P("fsdp", None),
        ),
        check_vma=False,
    )
```
